32 devices in a mesh: group: 2 (over y), scen: 4 (over z), site: 4 (over x, core).
Axes of the slice: x: 2, y: 2, z: 4, core: 2. Of those that a mesh axis runs over, the one named last changes fastest.
Arguments:
- dispatch: float32 [128, 256, 256], P(('group', 'scen'), 'site'), parts along dimension 0, may hold values from -6 to 6
- dual_price: float32 [128, 256, 256], P(('group', 'scen'), 'site'), parts along dimension 0, may hold values from -4 to 4
- net_load: bfloat16 [128, 256, 256], P(('group', 'scen'), 'site'), parts along dimension 0, may hold values from -6 to 6
- energy_price: float32 [512, 256], P(('group', 'site')), parts along dimension 0, may hold values from -4 to 4
- penalty: float32 [256], P('site'), may hold values from 0.5 to 2
- soc_weight: float32 [256], P('site'), may hold values from 2 to 20
- capacity: float32 [256], P('site'), may hold values from 1 to 3
- probability: float32 [128], P('group'), parts along dimension 0, may hold values from 0.3 to 9, as said below
- node_deep: int32 [128], P('group'), parts along dimension 0, may hold values from 0 to 7, never falling along the last dimension, each value on 1 to 16 neighbouring positions
Outputs:
- new_dispatch: float32 [128, 256, 256], P(('group', 'scen'), 'site'), parts along dimension 0
- new_dual: float32 [128, 256, 256], P(('group', 'scen'), 'site'), parts along dimension 0
The draws below stay inside these ranges and needn't reach their ends.
There are 2 independent parts, one for each index of `group`. The reference program is written for one: setup_inputs(seed, part) draws one part's arguments, and reference() takes and returns one part's arrays. A program takes and returns all parts, laid end to end along the dimension named above; an argument that names none is the same for every part. Nothing has to cross between parts.
Inputs may be any that keep to these rules, and one draw needn't show every extreme that they name: `probability`: scenario weights are positive. node_deep never falls along the scenarios; each node holds 1 to 16 scenarios, one exactly 16.
All inputs are finite; a program needn't handle non-finite values.
Results may differ from the reference program's by a relative error of at most 0.0003.
Values sent between devices are 32-bit elements; how exact they have to be, the bound alone decides.
A program may use at most 64 MiB of HBM per device.

```python
import math
import jax
import jax.numpy as jnp
import numpy as np

BRANCH = 4
MOST = 16
H = 256
SCENARIOS = 64
SITES = 256
NODES = 8


def draw_probability(key, part):
    order = jnp.arange(SCENARIOS, dtype=jnp.float32) / (SCENARIOS - 1)
    spread = jnp.exp(jax.random.uniform(key, (SCENARIOS,), jnp.float32, math.log(0.3), math.log(3.0)))
    return (1.0 + 2.0 * order) * spread


def block_levels(own_key, shape, cuts, smallest, top_value):
    def one(dim, blocks):
        steps = jax.random.uniform(jax.random.fold_in(jax.random.fold_in(own_key, 6), dim), (blocks,), jnp.float32, smallest / len(cuts), top_value / len(cuts))
        return jnp.repeat(jnp.exp(steps), shape[dim] // blocks).reshape((-1,) + (1,) * (len(shape) - dim - 1))

    factor_of = one(*cuts[0])
    for cut in cuts[1:]:
        factor_of = factor_of * one(*cut)
    return factor_of


def split_up(amount, total, most, slope):
    portions = [(1 << 20) // math.isqrt(rank ** slope) + 1 for rank in range(2, amount + 1)]
    spare, counts = total - most - (amount - 1), [1] * (amount - 1)
    while spare > 0:
        free = [i for i in range(amount - 1) if counts[i] < most]
        pool, budget = sum([portions[i] for i in free]), spare
        for i in free:
            addition = min(most - counts[i], max(1, budget * portions[i] // pool), spare)
            counts[i] = counts[i] + addition
            spare = spare - addition
    return np.array([most] + counts)


def ragged_sizes(own_key, amount, total, reach, lean):
    if amount == 2:
        one = jax.random.randint(own_key, (), max(1, total - reach), min(reach, total - 1) + 1)
        return jnp.stack([one, total - one])
    sizes = jnp.asarray(split_up(amount, total, reach, lean), jnp.int32)
    couples = (amount - 1) // 2
    giver, receiver = sizes[1:1 + 2 * couples:2], sizes[2:2 + 2 * couples:2]
    room = jnp.minimum(giver - 1, reach - receiver)
    shifted = jax.random.randint(jax.random.fold_in(own_key, 1), (couples,), 0, 1 << 20) % (room + 1)
    sizes = sizes.at[1:1 + 2 * couples:2].set(giver - shifted).at[2:2 + 2 * couples:2].set(receiver + shifted)
    return sizes[jax.random.permutation(jax.random.fold_in(own_key, 2), amount)]


def noise(stream_key, extent, scale, reach, shards=(), kind=jnp.bfloat16):
    array = scale * jax.random.normal(stream_key, extent, jnp.float32)
    if shards:
        array = array * block_levels(stream_key, extent, shards, -0.22, 0.18)
    return jnp.clip(array, -reach, reach).astype(kind)


def setup_inputs(seed: int = 0, part: int = 0) -> dict:
    arg_keys = jax.random.split(jax.random.key(seed), 10)
    part_splits = jax.random.split(jax.random.fold_in(arg_keys[9], part), 10)
    return {
        "dispatch": noise(part_splits[0], (SCENARIOS, SITES, H), 1.0, 6.0, ((0, 4), (1, 4)), jnp.float32),
        "dual_price": noise(part_splits[1], (SCENARIOS, SITES, H), 0.5, 4.0, ((0, 4), (1, 4)), jnp.float32),
        "net_load": noise(part_splits[2], (SCENARIOS, SITES, H), 1.0, 6.0, ((0, 4), (1, 4))),
        "energy_price": noise(part_splits[3], (SITES, H), 0.5, 4.0, ((0, 4),), jnp.float32),
        "penalty": jnp.clip(jnp.exp(math.log(2.0) - 1.3862944 * jax.random.uniform(arg_keys[4], (SITES,), jnp.float32) ** block_levels(arg_keys[4], (SITES,), ((0, 4),), -0.2, 0.2)), 0.5, 2.0),
        "soc_weight": jnp.clip(jnp.exp(math.log(20.0) - 2.3025851 * jax.random.uniform(arg_keys[5], (SITES,), jnp.float32) ** block_levels(arg_keys[5], (SITES,), ((0, 4),), -0.2, 0.2)), 2.0, 20.0),
        "capacity": jnp.clip(jnp.exp(math.log(3.0) - 1.0986123 * jax.random.uniform(arg_keys[6], (SITES,), jnp.float32) ** block_levels(arg_keys[6], (SITES,), ((0, 4),), -0.2, 0.2)), 1.0, 3.0),
        "probability": draw_probability(jax.random.fold_in(jax.random.fold_in(arg_keys[9], part), 71), part),
        "node_deep": jnp.searchsorted(jnp.cumsum(ragged_sizes(part_splits[8], NODES, SCENARIOS, MOST, 2)), jnp.arange(SCENARIOS), side="right").astype(jnp.int32),
    }


def node_average(values, weights, node_ids, node_count):
    sums = jax.ops.segment_sum(weights[:, None, None] * values, node_ids, num_segments=node_count)
    totals = jax.ops.segment_sum(weights, node_ids, num_segments=node_count)
    return sums[node_ids] / totals[node_ids][:, None, None]


def reference(dispatch, dual_price, net_load, energy_price, penalty, soc_weight, capacity, probability, node_deep):
    horizon = dispatch.shape[2]
    section_hours = horizon // 4
    upper_ids = node_deep // BRANCH
    root_ids = jnp.zeros_like(node_deep)
    levels = [(root_ids, 1), (upper_ids, NODES // BRANCH), (node_deep, NODES)]
    pieces = []
    for section_index in range(3):
        piece = dispatch[:, :, section_index * section_hours:(section_index + 1) * section_hours]
        pieces.append(node_average(piece, probability, levels[section_index][0], levels[section_index][1]))
    pieces.append(dispatch[:, :, 3 * section_hours:])
    node_mean = jnp.concatenate(pieces, axis=2)
    penalty_rate = penalty[None, :, None]
    new_dual = dual_price + penalty_rate * (dispatch - node_mean)
    step_size = 0.5 / (1.0 + penalty_rate)
    limit = capacity[None, :, None]
    charge_scale = soc_weight[None, :, None] / (horizon * horizon)
    load_float = net_load.astype(jnp.float32)
    current = dispatch
    for sweep_index in range(2):
        charge_state = jnp.cumsum(current, axis=2)
        ahead = jnp.flip(jnp.cumsum(jnp.flip(charge_state, 2), axis=2), 2)
        imbalance = jnp.sum(current - load_float, axis=1)
        gradient = (energy_price[None] + new_dual + penalty_rate * (current - node_mean)
                    + charge_scale * ahead + (2.0 / SITES) * imbalance[:, None, :])
        current = jnp.clip(current - step_size * gradient, -limit, limit)
    return current, new_dual
```

```python
import functools

import jax
import jax.numpy as jnp
from jax import lax
from jax.experimental import pallas as pl
from jax.experimental.pallas import tpu as pltpu
from jax.sharding import PartitionSpec as P

BRANCH = 4
MESH = pl.DeviceIdType.MESH
CHUNKS = 4


def kernel(
    n_scen,
    n_site,
    disp_hbm,
    dual_hbm,
    load_hbm,
    energy_hbm,
    pen_ref,
    soc_ref,
    cap_ref,
    prob_ref,
    node_ref,
    out_hbm,
    ndual_hbm,
    x_ref,
    dual_ref,
    load_ref,
    energy_ref,
    floc_ref,
    q_ref,
    z_ref,
    cur_ref,
    nd_ref,
    fin_ref,
    kern_ref,
    tab_ref,
    col_ref,
    pay_ref,
    payd_ref,
    got_ref,
    gotd_ref,
    imb_ref,
    imbr_ref,
    loadsum_ref,
    in_sem,
    out_sem,
    scen_send,
    scen_recv,
    deep_send,
    deep_recv,
    site_send,
    site_recv,
):
    scen_count, site_count, horizon = x_ref.shape
    hours = horizon // 4
    half = horizon // 2
    step_rows = scen_count // CHUNKS
    me = lax.axis_index("scen")
    here = lax.axis_index("site")

    def rows(c):
        return pl.ds(c * step_rows, step_rows)

    def fetch(c, which, src, dst):
        return pltpu.make_async_copy(src.at[rows(c)], dst.at[rows(c)], in_sem.at[which, c])

    ins = []
    for c in range(CHUNKS):
        ins.append((fetch(c, 0, disp_hbm, x_ref), fetch(c, 1, load_hbm, load_ref)))
        ins[c][0].start()
        ins[c][1].start()
    energy_in = pltpu.make_async_copy(energy_hbm, energy_ref, in_sem.at[3, 0])
    energy_in.start()
    dual_in = [fetch(c, 2, dual_hbm, dual_ref) for c in range(CHUNKS)]
    for c in range(CHUNKS):
        dual_in[c].start()

    @pl.when(me == 0)
    def _():
        gotd_ref[0] = jnp.zeros_like(gotd_ref[0])

    @pl.when(me == n_scen - 1)
    def _():
        gotd_ref[1] = jnp.zeros_like(gotd_ref[1])

    barrier = pltpu.get_barrier_semaphore()
    for j in range(1, n_scen):
        pl.semaphore_signal(
            barrier, inc=1, device_id={"scen": lax.rem(me + j, n_scen)}, device_id_type=MESH
        )
    for j in range(1, n_site):
        pl.semaphore_signal(
            barrier, inc=1, device_id={"site": lax.rem(here + j, n_site)}, device_id_type=MESH
        )

    total = prob_ref.shape[0]
    first_row = me * scen_count
    prob = prob_ref[...].reshape(1, total)
    node_int = node_ref[...].reshape(1, total)
    deep = node_int.astype(jnp.float32)
    upper = lax.div(node_int, jnp.full_like(node_int, BRANCH)).astype(jnp.float32)
    lane = lax.broadcasted_iota(jnp.int32, (scen_count, total), 1)
    sub = lax.broadcasted_iota(jnp.int32, (scen_count, total), 0)
    lane1 = lax.broadcasted_iota(jnp.int32, (1, total), 1)

    def pick(mask, row):
        return jnp.sum(jnp.where(mask, row, 0.0), axis=1, keepdims=True)

    own = lane == sub + first_row
    before = lane == sub + (first_row - 1)
    my_prob, my_deep, my_upper = pick(own, prob), pick(own, deep), pick(own, upper)
    first = lane1 == first_row
    last = lane1 == first_row + (scen_count - 1)
    first_deep, first_upper = pick(first, deep), pick(first, upper)
    last_deep, last_upper = pick(last, deep), pick(last, upper)

    def same(a, b):
        return jnp.where(a == b, 1.0, 0.0)

    section = lax.broadcasted_iota(jnp.int32, (scen_count, horizon), 1)

    def table(root, up, dp, leaf):
        return jnp.where(
            section < hours,
            root,
            jnp.where(section < 2 * hours, up, jnp.where(section < 3 * hours, dp, leaf)),
        )

    inv_root = 1.0 / jnp.sum(prob, axis=1, keepdims=True)
    inv_upper = 1.0 / pick(my_upper == upper, prob)
    inv_deep = 1.0 / pick(my_deep == deep, prob)
    inv = table(inv_root, inv_upper, inv_deep, 1.0)
    from_left = table(1.0, same(my_upper, first_upper), same(my_deep, first_deep), 0.0)
    from_right = table(1.0, same(my_upper, last_upper), same(my_deep, last_deep), 0.0)
    tab_ref[0] = table(my_prob, my_prob, my_prob, 1.0)
    tab_ref[1] = table(
        1.0, same(my_upper, pick(before, upper)), same(my_deep, pick(before, deep)), 0.0
    )
    tab_ref[2] = from_left
    tab_ref[3] = inv
    tab_ref[4] = inv * from_left
    tab_ref[5] = inv * from_right

    eye = lax.broadcasted_iota(jnp.int32, (site_count, site_count), 0) == (
        lax.broadcasted_iota(jnp.int32, (site_count, site_count), 1)
    )

    def column(ref):
        return pick(eye, ref[...].reshape(1, site_count))

    pen = column(pen_ref)
    step = 0.5 / (1.0 + pen)
    wide = (site_count, horizon)
    sites_all = site_count * n_site
    col_ref[0] = jnp.broadcast_to(pen, wide)
    col_ref[1] = jnp.broadcast_to(step, wide)
    col_ref[2] = jnp.broadcast_to(step * column(soc_ref) / (horizon * horizon), wide)
    col_ref[3] = jnp.broadcast_to(step * (2.0 / sites_all), wide)
    col_ref[4] = jnp.broadcast_to(column(cap_ref), wide)
    hour_a = lax.broadcasted_iota(jnp.int32, (horizon, horizon), 0)
    hour_b = lax.broadcasted_iota(jnp.int32, (horizon, horizon), 1)
    kern_ref[...] = (horizon - jnp.maximum(hour_a, hour_b)).astype(jnp.float32).astype(kern_ref.dtype)

    def ahead_of(ref, c):
        flat = ref[rows(c)].reshape(step_rows * site_count, horizon)
        if kern_ref.dtype == jnp.bfloat16:
            high = flat.astype(jnp.bfloat16)
            low = (flat - high.astype(jnp.float32)).astype(jnp.bfloat16)
            ahead = jnp.dot(high, kern_ref[...], preferred_element_type=jnp.float32) + jnp.dot(
                low, kern_ref[...], preferred_element_type=jnp.float32
            )
        else:
            ahead = jnp.dot(flat, kern_ref[...], precision=lax.Precision.HIGHEST)
        return ahead.reshape(step_rows, site_count, horizon)

    def row(ref, s):
        return ref[pl.ds(s, 1), :]

    fore = None
    first_sum = None
    for c in range(CHUNKS):
        ins[c][0].wait()
        ins[c][1].wait()
        for s in range(c * step_rows, (c + 1) * step_rows):
            x = x_ref[s]
            load_total = jnp.sum(load_ref[s].astype(jnp.float32), axis=0, keepdims=True)
            loadsum_ref[pl.ds(s, 1), :] = load_total
            imb_ref[0, pl.ds(s, 1), :] = jnp.sum(x, axis=0, keepdims=True) - load_total
            weighted = x * row(tab_ref.at[0], s)
            fore = weighted if fore is None else weighted + row(tab_ref.at[1], s) * fore
            floc_ref[s] = fore
            part = weighted * row(tab_ref.at[2], s)
            first_sum = part if first_sum is None else first_sum + part

    half_lane = lax.broadcasted_iota(jnp.int32, (site_count // 2, half), 1)

    def fill(slot, value):
        pay_ref[slot] = value[:, :half]
        tail = value[:, half:]
        payd_ref[slot] = jnp.where(
            half_lane < hours,
            tail[: site_count // 2],
            pltpu.roll(tail[site_count // 2 :], hours, axis=1),
        )

    fill(0, fore)
    fill(1, first_sum)

    pl.semaphore_wait(barrier, n_scen + n_site - 2)

    scen_copies = []
    for j in range(1, n_scen):
        peer = lax.rem(me + j, n_scen)
        side = jnp.where(peer > me, 0, 1)
        scen_copies.append(
            pltpu.make_async_remote_copy(
                src_ref=pay_ref.at[side],
                dst_ref=got_ref.at[j - 1],
                send_sem=scen_send.at[j - 1],
                recv_sem=scen_recv.at[j - 1],
                device_id={"scen": peer},
                device_id_type=MESH,
            )
        )
    deep_copies = []
    for side, peer in ((0, jnp.minimum(me + 1, n_scen - 1)), (1, jnp.maximum(me - 1, 0))):
        deep_copies.append(
            pltpu.make_async_remote_copy(
                src_ref=payd_ref.at[side],
                dst_ref=gotd_ref.at[side],
                send_sem=deep_send.at[side],
                recv_sem=deep_recv.at[side],
                device_id={"scen": peer},
                device_id_type=MESH,
            )
        )
    has_right = me < n_scen - 1
    has_left = me > 0

    def site_copies(turn):
        return [
            pltpu.make_async_remote_copy(
                src_ref=imb_ref.at[turn],
                dst_ref=imbr_ref.at[turn, j - 1],
                send_sem=site_send.at[turn, j - 1],
                recv_sem=site_recv.at[turn, j - 1],
                device_id={"site": lax.rem(here + j, n_site)},
                device_id_type=MESH,
            )
            for j in range(1, n_site)
        ]

    for copy in scen_copies:
        copy.start()

    @pl.when(has_right)
    def _():
        deep_copies[0].start()

    @pl.when(has_left)
    def _():
        deep_copies[1].start()

    sites_first = site_copies(0)
    for copy in sites_first:
        copy.start()

    energy_in.wait()
    fin_ref[0] = col_ref[1] * energy_ref[...]
    back = None
    for s in reversed(range(scen_count)):
        if back is None:
            back = floc_ref[s]
        else:
            back = jnp.where(row(tab_ref.at[1], s + 1) > 0.5, back, floc_ref[s])
        q_ref[s] = col_ref[0] * (x_ref[s] - back * row(tab_ref.at[3], s))
    for c in range(CHUNKS):
        ahead = ahead_of(x_ref, c)
        dual_in[c].wait()
        for i in range(step_rows):
            s = c * step_rows + i
            z_ref[s] = x_ref[s] - fin_ref[0] - col_ref[1] * dual_ref[s] - col_ref[2] * ahead[i]

    left = jnp.zeros((site_count, half), jnp.float32)
    right = jnp.zeros((site_count, half), jnp.float32)
    front_lane = lax.broadcasted_iota(jnp.int32, (1, half), 1)
    gates = []
    for j in range(1, n_scen):
        peer = lax.rem(me + (n_scen - j), n_scen)
        peer_last = lane1 == peer * scen_count + (scen_count - 1)
        peer_first = lane1 == peer * scen_count
        is_left = jnp.where(peer < me, 1.0, 0.0)
        gates.append(
            (
                is_left * jnp.where(front_lane < hours, 1.0, same(pick(peer_last, upper), first_upper)),
                (1.0 - is_left)
                * jnp.where(front_lane < hours, 1.0, same(pick(peer_first, upper), last_upper)),
            )
        )
    gate_left = same(pick(lane1 == first_row - 1, deep), first_deep)
    gate_right = same(pick(lane1 == first_row + scen_count, deep), last_deep)

    def unpack(value):
        return jnp.concatenate([value, pltpu.roll(value, hours, axis=1)], axis=0)

    for copy in sites_first:
        copy.wait_recv()
    imb_one = imb_ref[0]
    for j in range(n_site - 1):
        imb_one = imb_one + imbr_ref[0, j]
    tab_ref[0] = imb_one

    @pl.when(has_left)
    def _():
        deep_copies[0].wait_recv()

    @pl.when(has_right)
    def _():
        deep_copies[1].wait_recv()

    for j in range(1, n_scen):
        scen_copies[j - 1].wait_recv()
        got = got_ref[j - 1]
        left = left + gates[j - 1][0] * got
        right = right + gates[j - 1][1] * got
    fin_ref[1] = col_ref[0] * jnp.concatenate([left, gate_left * unpack(gotd_ref[0])], axis=1)
    fin_ref[2] = col_ref[0] * jnp.concatenate([right, gate_right * unpack(gotd_ref[1])], axis=1)

    for s in range(scen_count):
        q = (
            q_ref[s]
            - row(tab_ref.at[4], s) * fin_ref[1]
            - row(tab_ref.at[5], s) * fin_ref[2]
        )
        nd_ref[s] = dual_ref[s] + q
        cap = col_ref[4]
        new = z_ref[s] - 2.0 * col_ref[1] * q - col_ref[3] * row(tab_ref.at[0], s)
        new = jnp.minimum(jnp.maximum(new, -cap), cap)
        cur_ref[s] = new
        imb_ref[1, pl.ds(s, 1), :] = jnp.sum(new, axis=0, keepdims=True) - row(loadsum_ref, s)

    sites_second = site_copies(1)
    for copy in sites_second:
        copy.start()
    dual_out = pltpu.make_async_copy(nd_ref, ndual_hbm, out_sem.at[0])
    dual_out.start()

    for c in range(CHUNKS):
        ahead = ahead_of(cur_ref, c)
        for i in range(step_rows):
            s = c * step_rows + i
            now = cur_ref[s]
            z_ref[s] = (
                now
                - fin_ref[0]
                - col_ref[1]
                * (2.0 * nd_ref[s] - dual_ref[s] + col_ref[0] * (now - x_ref[s]))
                - col_ref[2] * ahead[i]
            )

    for copy in sites_second:
        copy.wait_recv()
    imb_two = imb_ref[1]
    for j in range(n_site - 1):
        imb_two = imb_two + imbr_ref[1, j]
    tab_ref[1] = imb_two
    outs = []
    for c in range(CHUNKS):
        for i in range(step_rows):
            s = c * step_rows + i
            cap = col_ref[4]
            new = z_ref[s] - col_ref[3] * row(tab_ref.at[1], s)
            q_ref[s] = jnp.minimum(jnp.maximum(new, -cap), cap)
        copy = pltpu.make_async_copy(q_ref.at[rows(c)], out_hbm.at[rows(c)], out_sem.at[c + 1])
        copy.start()
        outs.append(copy)

    for copy in scen_copies + sites_first + sites_second:
        copy.wait_send()

    @pl.when(has_right)
    def _():
        deep_copies[0].wait_send()

    @pl.when(has_left)
    def _():
        deep_copies[1].wait_send()

    dual_out.wait()
    for copy in outs:
        copy.wait()


def body(
    n_scen,
    n_site,
    dispatch,
    dual_price,
    net_load,
    energy_price,
    penalty,
    soc_weight,
    capacity,
    probability,
    node_deep,
):
    scen_count, site_count, horizon = dispatch.shape
    f32 = jnp.float32
    full = (scen_count, site_count, horizon)
    half = horizon // 2
    vmem = pltpu.VMEM
    any_spec = pl.BlockSpec(memory_space=pl.ANY)
    vmem_spec = pl.BlockSpec(memory_space=vmem)
    kern_type = jnp.bfloat16 if horizon <= 256 else f32
    dma = pltpu.SemaphoreType.DMA
    return pl.pallas_call(
        functools.partial(kernel, n_scen, n_site),
        out_shape=(jax.ShapeDtypeStruct(full, f32), jax.ShapeDtypeStruct(full, f32)),
        in_specs=[any_spec] * 4 + [vmem_spec] * 5,
        out_specs=(any_spec, any_spec),
        scratch_shapes=[
            vmem(full, f32),
            vmem(full, f32),
            vmem(full, net_load.dtype),
            vmem((site_count, horizon), f32),
            vmem(full, f32),
            vmem(full, f32),
            vmem(full, f32),
            vmem(full, f32),
            vmem(full, f32),
            vmem((3, site_count, horizon), f32),
            vmem((horizon, horizon), kern_type),
            vmem((6, scen_count, horizon), f32),
            vmem((5, site_count, horizon), f32),
            vmem((2, site_count, half), f32),
            vmem((2, site_count // 2, half), f32),
            vmem((n_scen - 1, site_count, half), f32),
            vmem((2, site_count // 2, half), f32),
            vmem((2, scen_count, horizon), f32),
            vmem((2, n_site - 1, scen_count, horizon), f32),
            vmem((scen_count, horizon), f32),
            dma((4, CHUNKS)),
            dma((CHUNKS + 1,)),
            dma((n_scen - 1,)),
            dma((n_scen - 1,)),
            dma((2,)),
            dma((2,)),
            dma((2, n_site - 1)),
            dma((2, n_site - 1)),
        ],
        compiler_params=pltpu.CompilerParams(
            collective_id=0, has_side_effects=True, vmem_limit_bytes=48 * 1024 * 1024
        ),
    )(
        dispatch,
        dual_price,
        net_load,
        energy_price,
        penalty,
        soc_weight,
        capacity,
        probability,
        node_deep,
    )


def solution(mesh):
    in_specs = (
        P(("group", "scen"), "site", None),
        P(("group", "scen"), "site", None),
        P(("group", "scen"), "site", None),
        P(("group", "site"), None),
        P("site"),
        P("site"),
        P("site"),
        P("group"),
        P("group"),
    )
    out_specs = (P(("group", "scen"), "site", None), P(("group", "scen"), "site", None))
    return jax.shard_map(
        functools.partial(body, mesh.shape["scen"], mesh.shape["site"]),
        mesh=mesh,
        in_specs=in_specs,
        out_specs=out_specs,
        check_vma=False,
    )
```

```python
import functools

import jax
import jax.numpy as jnp
from jax import lax
from jax.experimental import pallas as pl
from jax.experimental.pallas import tpu as pltpu
from jax.sharding import PartitionSpec as P

BRANCH = 4
MESH = pl.DeviceIdType.MESH
CHUNKS = 4


def kernel(
    n_scen,
    n_site,
    disp_hbm,
    dual_hbm,
    load_hbm,
    energy_hbm,
    pen_hbm,
    soc_hbm,
    cap_hbm,
    prob_hbm,
    node_hbm,
    z_ref,
    nd_ref,
    imb_out,
    col_out,
    pen_ref,
    soc_ref,
    cap_ref,
    prob_ref,
    node_ref,
    x_ref,
    dual_ref,
    load_ref,
    energy_ref,
    floc_ref,
    q_ref,
    cur_ref,
    fin_ref,
    kern_ref,
    tab_ref,
    col_ref,
    pay_ref,
    payd_ref,
    got_ref,
    gotd_ref,
    imb_ref,
    imbr_ref,
    loadsum_ref,
    in_sem,
    small_sem,
    scen_send,
    scen_recv,
    deep_send,
    deep_recv,
    site_send,
    site_recv,
):
    scen_count, site_count, horizon = x_ref.shape
    hours = horizon // 4
    half = horizon // 2
    step_rows = scen_count // CHUNKS
    me = lax.axis_index("scen")
    here = lax.axis_index("site")

    def rows(c):
        return pl.ds(c * step_rows, step_rows)

    def fetch(c, which, src, dst):
        return pltpu.make_async_copy(src.at[rows(c)], dst.at[rows(c)], in_sem.at[which, c])

    smalls = [
        pltpu.make_async_copy(src, dst, small_sem.at[i])
        for i, (src, dst) in enumerate(
            (
                (prob_hbm, prob_ref),
                (node_hbm, node_ref),
                (pen_hbm, pen_ref),
                (soc_hbm, soc_ref),
                (cap_hbm, cap_ref),
            )
        )
    ]
    for copy in smalls:
        copy.start()
    ins = []
    for c in range(CHUNKS):
        ins.append((fetch(c, 0, disp_hbm, x_ref), fetch(c, 1, load_hbm, load_ref)))
        ins[c][0].start()
        ins[c][1].start()
    energy_in = pltpu.make_async_copy(energy_hbm, energy_ref, in_sem.at[3, 0])
    energy_in.start()
    dual_in = [fetch(c, 2, dual_hbm, dual_ref) for c in range(CHUNKS)]
    for c in range(CHUNKS):
        dual_in[c].start()

    @pl.when(me == 0)
    def _():
        gotd_ref[0] = jnp.zeros_like(gotd_ref[0])

    @pl.when(me == n_scen - 1)
    def _():
        gotd_ref[1] = jnp.zeros_like(gotd_ref[1])

    barrier = pltpu.get_barrier_semaphore()
    for j in range(1, n_scen):
        pl.semaphore_signal(
            barrier, inc=1, device_id={"scen": lax.rem(me + j, n_scen)}, device_id_type=MESH
        )
    for j in range(1, n_site):
        pl.semaphore_signal(
            barrier, inc=1, device_id={"site": lax.rem(here + j, n_site)}, device_id_type=MESH
        )

    for copy in smalls:
        copy.wait()

    total = prob_ref.shape[0]
    first_row = me * scen_count
    prob = prob_ref[...].reshape(1, total)
    node_int = node_ref[...].reshape(1, total)
    deep = node_int.astype(jnp.float32)
    upper = lax.div(node_int, jnp.full_like(node_int, BRANCH)).astype(jnp.float32)
    lane = lax.broadcasted_iota(jnp.int32, (scen_count, total), 1)
    sub = lax.broadcasted_iota(jnp.int32, (scen_count, total), 0)
    lane1 = lax.broadcasted_iota(jnp.int32, (1, total), 1)

    def pick(mask, row):
        return jnp.sum(jnp.where(mask, row, 0.0), axis=1, keepdims=True)

    own = lane == sub + first_row
    before = lane == sub + (first_row - 1)
    my_prob, my_deep, my_upper = pick(own, prob), pick(own, deep), pick(own, upper)
    first = lane1 == first_row
    last = lane1 == first_row + (scen_count - 1)
    first_deep, first_upper = pick(first, deep), pick(first, upper)
    last_deep, last_upper = pick(last, deep), pick(last, upper)

    def same(a, b):
        return jnp.where(a == b, 1.0, 0.0)

    section = lax.broadcasted_iota(jnp.int32, (scen_count, horizon), 1)

    def table(root, up, dp, leaf):
        return jnp.where(
            section < hours,
            root,
            jnp.where(section < 2 * hours, up, jnp.where(section < 3 * hours, dp, leaf)),
        )

    inv_root = 1.0 / jnp.sum(prob, axis=1, keepdims=True)
    inv_upper = 1.0 / pick(my_upper == upper, prob)
    inv_deep = 1.0 / pick(my_deep == deep, prob)
    inv = table(inv_root, inv_upper, inv_deep, 1.0)
    from_left = table(1.0, same(my_upper, first_upper), same(my_deep, first_deep), 0.0)
    from_right = table(1.0, same(my_upper, last_upper), same(my_deep, last_deep), 0.0)
    tab_ref[0] = table(my_prob, my_prob, my_prob, 1.0)
    tab_ref[1] = table(
        1.0, same(my_upper, pick(before, upper)), same(my_deep, pick(before, deep)), 0.0
    )
    tab_ref[2] = from_left
    tab_ref[3] = inv
    tab_ref[4] = inv * from_left
    tab_ref[5] = inv * from_right

    eye = lax.broadcasted_iota(jnp.int32, (site_count, site_count), 0) == (
        lax.broadcasted_iota(jnp.int32, (site_count, site_count), 1)
    )

    def column(ref):
        return pick(eye, ref[...].reshape(1, site_count))

    pen = column(pen_ref)
    step = 0.5 / (1.0 + pen)
    wide = (site_count, horizon)
    sites_all = site_count * n_site
    col_ref[0] = jnp.broadcast_to(pen, wide)
    col_ref[1] = jnp.broadcast_to(step, wide)
    col_ref[2] = jnp.broadcast_to(step * column(soc_ref) / (horizon * horizon), wide)
    col_out[0] = jnp.broadcast_to(step * (2.0 / sites_all), wide)
    col_out[1] = jnp.broadcast_to(column(cap_ref), wide)
    hour_a = lax.broadcasted_iota(jnp.int32, (horizon, horizon), 0)
    hour_b = lax.broadcasted_iota(jnp.int32, (horizon, horizon), 1)
    kern_ref[...] = (horizon - jnp.maximum(hour_a, hour_b)).astype(jnp.float32).astype(kern_ref.dtype)

    def ahead_of(ref, c):
        flat = ref[rows(c)].reshape(step_rows * site_count, horizon)
        if kern_ref.dtype == jnp.bfloat16:
            high = flat.astype(jnp.bfloat16)
            low = (flat - high.astype(jnp.float32)).astype(jnp.bfloat16)
            ahead = jnp.dot(high, kern_ref[...], preferred_element_type=jnp.float32) + jnp.dot(
                low, kern_ref[...], preferred_element_type=jnp.float32
            )
        else:
            ahead = jnp.dot(flat, kern_ref[...], precision=lax.Precision.HIGHEST)
        return ahead.reshape(step_rows, site_count, horizon)

    def row(ref, s):
        return ref[pl.ds(s, 1), :]

    fore = None
    first_sum = None
    for c in range(CHUNKS):
        ins[c][0].wait()
        ins[c][1].wait()
        for s in range(c * step_rows, (c + 1) * step_rows):
            x = x_ref[s]
            load_total = jnp.sum(load_ref[s].astype(jnp.float32), axis=0, keepdims=True)
            loadsum_ref[pl.ds(s, 1), :] = load_total
            imb_ref[0, pl.ds(s, 1), :] = jnp.sum(x, axis=0, keepdims=True) - load_total
            weighted = x * row(tab_ref.at[0], s)
            fore = weighted if fore is None else weighted + row(tab_ref.at[1], s) * fore
            floc_ref[s] = fore
            part = weighted * row(tab_ref.at[2], s)
            first_sum = part if first_sum is None else first_sum + part

    half_lane = lax.broadcasted_iota(jnp.int32, (site_count // 2, half), 1)

    def fill(slot, value):
        pay_ref[slot] = value[:, :half]
        tail = value[:, half:]
        payd_ref[slot] = jnp.where(
            half_lane < hours,
            tail[: site_count // 2],
            pltpu.roll(tail[site_count // 2 :], hours, axis=1),
        )

    fill(0, fore)
    fill(1, first_sum)

    pl.semaphore_wait(barrier, n_scen + n_site - 2)

    scen_copies = []
    for j in range(1, n_scen):
        peer = lax.rem(me + j, n_scen)
        side = jnp.where(peer > me, 0, 1)
        scen_copies.append(
            pltpu.make_async_remote_copy(
                src_ref=pay_ref.at[side],
                dst_ref=got_ref.at[j - 1],
                send_sem=scen_send.at[j - 1],
                recv_sem=scen_recv.at[j - 1],
                device_id={"scen": peer},
                device_id_type=MESH,
            )
        )
    deep_copies = []
    for side, peer in ((0, jnp.minimum(me + 1, n_scen - 1)), (1, jnp.maximum(me - 1, 0))):
        deep_copies.append(
            pltpu.make_async_remote_copy(
                src_ref=payd_ref.at[side],
                dst_ref=gotd_ref.at[side],
                send_sem=deep_send.at[side],
                recv_sem=deep_recv.at[side],
                device_id={"scen": peer},
                device_id_type=MESH,
            )
        )
    has_right = me < n_scen - 1
    has_left = me > 0

    def site_copies(turn):
        return [
            pltpu.make_async_remote_copy(
                src_ref=imb_ref.at[turn],
                dst_ref=imbr_ref.at[turn, j - 1],
                send_sem=site_send.at[turn, j - 1],
                recv_sem=site_recv.at[turn, j - 1],
                device_id={"site": lax.rem(here + j, n_site)},
                device_id_type=MESH,
            )
            for j in range(1, n_site)
        ]

    for copy in scen_copies:
        copy.start()

    @pl.when(has_right)
    def _():
        deep_copies[0].start()

    @pl.when(has_left)
    def _():
        deep_copies[1].start()

    sites_first = site_copies(0)
    for copy in sites_first:
        copy.start()

    energy_in.wait()
    fin_ref[0] = col_ref[1] * energy_ref[...]
    back = None
    for s in reversed(range(scen_count)):
        if back is None:
            back = floc_ref[s]
        else:
            back = jnp.where(row(tab_ref.at[1], s + 1) > 0.5, back, floc_ref[s])
        q_ref[s] = col_ref[0] * (x_ref[s] - back * row(tab_ref.at[3], s))
    for c in range(CHUNKS):
        ahead = ahead_of(x_ref, c)
        dual_in[c].wait()
        for i in range(step_rows):
            s = c * step_rows + i
            z_ref[s] = x_ref[s] - fin_ref[0] - col_ref[1] * dual_ref[s] - col_ref[2] * ahead[i]

    left = jnp.zeros((site_count, half), jnp.float32)
    right = jnp.zeros((site_count, half), jnp.float32)
    front_lane = lax.broadcasted_iota(jnp.int32, (1, half), 1)
    gates = []
    for j in range(1, n_scen):
        peer = lax.rem(me + (n_scen - j), n_scen)
        peer_last = lane1 == peer * scen_count + (scen_count - 1)
        peer_first = lane1 == peer * scen_count
        is_left = jnp.where(peer < me, 1.0, 0.0)
        gates.append(
            (
                is_left * jnp.where(front_lane < hours, 1.0, same(pick(peer_last, upper), first_upper)),
                (1.0 - is_left)
                * jnp.where(front_lane < hours, 1.0, same(pick(peer_first, upper), last_upper)),
            )
        )
    gate_left = same(pick(lane1 == first_row - 1, deep), first_deep)
    gate_right = same(pick(lane1 == first_row + scen_count, deep), last_deep)

    def unpack(value):
        return jnp.concatenate([value, pltpu.roll(value, hours, axis=1)], axis=0)

    for copy in sites_first:
        copy.wait_recv()
    imb_one = imb_ref[0]
    for j in range(n_site - 1):
        imb_one = imb_one + imbr_ref[0, j]
    tab_ref[0] = imb_one

    @pl.when(has_left)
    def _():
        deep_copies[0].wait_recv()

    @pl.when(has_right)
    def _():
        deep_copies[1].wait_recv()

    for j in range(1, n_scen):
        scen_copies[j - 1].wait_recv()
        got = got_ref[j - 1]
        left = left + gates[j - 1][0] * got
        right = right + gates[j - 1][1] * got
    fin_ref[1] = col_ref[0] * jnp.concatenate([left, gate_left * unpack(gotd_ref[0])], axis=1)
    fin_ref[2] = col_ref[0] * jnp.concatenate([right, gate_right * unpack(gotd_ref[1])], axis=1)

    for s in range(scen_count):
        q = (
            q_ref[s]
            - row(tab_ref.at[4], s) * fin_ref[1]
            - row(tab_ref.at[5], s) * fin_ref[2]
        )
        nd_ref[s] = dual_ref[s] + q
        cap = col_out[1]
        new = z_ref[s] - 2.0 * col_ref[1] * q - col_out[0] * row(tab_ref.at[0], s)
        new = jnp.minimum(jnp.maximum(new, -cap), cap)
        cur_ref[s] = new
        imb_ref[1, pl.ds(s, 1), :] = jnp.sum(new, axis=0, keepdims=True) - row(loadsum_ref, s)

    sites_second = site_copies(1)
    for copy in sites_second:
        copy.start()

    for c in range(CHUNKS):
        ahead = ahead_of(cur_ref, c)
        for i in range(step_rows):
            s = c * step_rows + i
            now = cur_ref[s]
            z_ref[s] = (
                now
                - fin_ref[0]
                - col_ref[1]
                * (2.0 * nd_ref[s] - dual_ref[s] + col_ref[0] * (now - x_ref[s]))
                - col_ref[2] * ahead[i]
            )

    for copy in sites_second:
        copy.wait_recv()
    imb_two = imb_ref[1]
    for j in range(n_site - 1):
        imb_two = imb_two + imbr_ref[1, j]
    imb_out[...] = imb_two

    for copy in scen_copies + sites_first + sites_second:
        copy.wait_send()

    @pl.when(has_right)
    def _():
        deep_copies[0].wait_send()

    @pl.when(has_left)
    def _():
        deep_copies[1].wait_send()


def finish(z_ref, nd_ref, imb_ref, col_ref, out_hbm, ndual_hbm, new_ref, out_sem):
    scen_count = z_ref.shape[0]
    step_rows = scen_count // CHUNKS
    outs = [pltpu.make_async_copy(nd_ref, ndual_hbm, out_sem.at[CHUNKS])]
    outs[0].start()
    cap = col_ref[1]
    for c in range(CHUNKS):
        for s in range(c * step_rows, (c + 1) * step_rows):
            new = z_ref[s] - col_ref[0] * imb_ref[pl.ds(s, 1), :]
            new_ref[s] = jnp.minimum(jnp.maximum(new, -cap), cap)
        part = pl.ds(c * step_rows, step_rows)
        copy = pltpu.make_async_copy(new_ref.at[part], out_hbm.at[part], out_sem.at[c])
        copy.start()
        outs.append(copy)
    for copy in outs:
        copy.wait()


def body(
    n_scen,
    n_site,
    dispatch,
    dual_price,
    net_load,
    energy_price,
    penalty,
    soc_weight,
    capacity,
    probability,
    node_deep,
):
    scen_count, site_count, horizon = dispatch.shape
    f32 = jnp.float32
    full = (scen_count, site_count, horizon)
    half = horizon // 2
    vmem = pltpu.VMEM
    hbm_spec = pl.BlockSpec(memory_space=pltpu.HBM)
    vmem_spec = pl.BlockSpec(memory_space=vmem)
    kern_type = jnp.bfloat16 if horizon <= 256 else f32
    dma = pltpu.SemaphoreType.DMA
    shape = jax.ShapeDtypeStruct
    big = [
        pltpu.with_memory_space_constraint(x, pltpu.HBM)
        for x in (dispatch, dual_price, net_load, energy_price, penalty, soc_weight, capacity, probability, node_deep)
    ]
    parts = pl.pallas_call(
        functools.partial(kernel, n_scen, n_site),
        out_shape=(
            shape(full, f32),
            shape(full, f32),
            shape((scen_count, horizon), f32),
            shape((2, site_count, horizon), f32),
        ),
        in_specs=[hbm_spec] * 9,
        out_specs=(vmem_spec,) * 4,
        scratch_shapes=[
            vmem(penalty.shape, f32),
            vmem(penalty.shape, f32),
            vmem(penalty.shape, f32),
            vmem(probability.shape, f32),
            vmem(node_deep.shape, node_deep.dtype),
            vmem(full, f32),
            vmem(full, f32),
            vmem(full, net_load.dtype),
            vmem((site_count, horizon), f32),
            vmem(full, f32),
            vmem(full, f32),
            vmem(full, f32),
            vmem((3, site_count, horizon), f32),
            vmem((horizon, horizon), kern_type),
            vmem((6, scen_count, horizon), f32),
            vmem((3, site_count, horizon), f32),
            vmem((2, site_count, half), f32),
            vmem((2, site_count // 2, half), f32),
            vmem((n_scen - 1, site_count, half), f32),
            vmem((2, site_count // 2, half), f32),
            vmem((2, scen_count, horizon), f32),
            vmem((2, n_site - 1, scen_count, horizon), f32),
            vmem((scen_count, horizon), f32),
            dma((4, CHUNKS)),
            dma((5,)),
            dma((n_scen - 1,)),
            dma((n_scen - 1,)),
            dma((2,)),
            dma((2,)),
            dma((2, n_site - 1)),
            dma((2, n_site - 1)),
        ],
        compiler_params=pltpu.CompilerParams(
            collective_id=0, has_side_effects=True, vmem_limit_bytes=24 * 1024 * 1024
        ),
    )(*big)
    return pl.pallas_call(
        finish,
        out_shape=(shape(full, f32), shape(full, f32)),
        in_specs=[vmem_spec] * 4,
        out_specs=(hbm_spec, hbm_spec),
        scratch_shapes=[vmem(full, f32), dma((CHUNKS + 1,))],
        compiler_params=pltpu.CompilerParams(vmem_limit_bytes=24 * 1024 * 1024),
    )(*parts)


def solution(mesh):
    in_specs = (
        P(("group", "scen"), "site", None),
        P(("group", "scen"), "site", None),
        P(("group", "scen"), "site", None),
        P(("group", "site"), None),
        P("site"),
        P("site"),
        P("site"),
        P("group"),
        P("group"),
    )
    out_specs = (P(("group", "scen"), "site", None), P(("group", "scen"), "site", None))
    return jax.shard_map(
        functools.partial(body, mesh.shape["scen"], mesh.shape["site"]),
        mesh=mesh,
        in_specs=in_specs,
        out_specs=out_specs,
        check_vma=False,
    )
```

```python
import functools

import jax
import jax.numpy as jnp
from jax import lax
from jax.experimental import pallas as pl
from jax.experimental.pallas import tpu as pltpu
from jax.sharding import PartitionSpec as P

BRANCH = 4
MESH = pl.DeviceIdType.MESH
CHUNKS = 4


def kernel(
    n_scen,
    n_site,
    disp_hbm,
    dual_hbm,
    load_hbm,
    energy_hbm,
    pen_hbm,
    soc_hbm,
    cap_hbm,
    prob_hbm,
    node_hbm,
    z_ref,
    nd_ref,
    imb_out,
    col_out,
    pen_ref,
    soc_ref,
    cap_ref,
    prob_ref,
    node_ref,
    x_ref,
    dual_ref,
    load_ref,
    energy_ref,
    floc_ref,
    q_ref,
    cur_ref,
    fin_ref,
    kern_ref,
    tab_ref,
    col_ref,
    pay_ref,
    payd_ref,
    got_ref,
    gotd_ref,
    imb_ref,
    imbr_ref,
    loadsum_ref,
    in_sem,
    small_sem,
    scen_send,
    scen_recv,
    deep_send,
    deep_recv,
    site_send,
    site_recv,
):
    scen_count, site_count, horizon = x_ref.shape
    hours = horizon // 4
    half = horizon // 2
    step_rows = scen_count // CHUNKS
    me = lax.axis_index("scen")
    here = lax.axis_index("site")

    def rows(c):
        return pl.ds(c * step_rows, step_rows)

    def fetch(c, which, src, dst):
        return pltpu.make_async_copy(src.at[rows(c)], dst.at[rows(c)], in_sem.at[which, c])

    barrier = pltpu.get_barrier_semaphore()
    for j in range(1, n_scen):
        pl.semaphore_signal(
            barrier, inc=1, device_id={"scen": lax.rem(me + j, n_scen)}, device_id_type=MESH
        )
    for j in range(1, n_site):
        pl.semaphore_signal(
            barrier, inc=1, device_id={"site": lax.rem(here + j, n_site)}, device_id_type=MESH
        )


    smalls = [
        pltpu.make_async_copy(src, dst, small_sem.at[i])
        for i, (src, dst) in enumerate(
            (
                (prob_hbm, prob_ref),
                (node_hbm, node_ref),
                (pen_hbm, pen_ref),
                (soc_hbm, soc_ref),
                (cap_hbm, cap_ref),
            )
        )
    ]
    for copy in smalls:
        copy.start()
    ins = []
    for c in range(CHUNKS):
        ins.append((fetch(c, 0, disp_hbm, x_ref), fetch(c, 1, load_hbm, load_ref)))
        ins[c][0].start()
    for c in range(CHUNKS):
        ins[c][1].start()
    energy_in = pltpu.make_async_copy(energy_hbm, energy_ref, in_sem.at[3, 0])
    energy_in.start()
    dual_in = [fetch(c, 2, dual_hbm, dual_ref) for c in range(CHUNKS)]
    for c in range(CHUNKS):
        dual_in[c].start()

    @pl.when(me == 0)
    def _():
        gotd_ref[0] = jnp.zeros_like(gotd_ref[0])

    @pl.when(me == n_scen - 1)
    def _():
        gotd_ref[1] = jnp.zeros_like(gotd_ref[1])

    for copy in smalls:
        copy.wait()

    total = prob_ref.shape[0]
    first_row = me * scen_count
    prob = prob_ref[...].reshape(1, total)
    node_int = node_ref[...].reshape(1, total)
    deep = node_int.astype(jnp.float32)
    upper = lax.div(node_int, jnp.full_like(node_int, BRANCH)).astype(jnp.float32)
    lane = lax.broadcasted_iota(jnp.int32, (scen_count, total), 1)
    sub = lax.broadcasted_iota(jnp.int32, (scen_count, total), 0)
    lane1 = lax.broadcasted_iota(jnp.int32, (1, total), 1)

    def pick(mask, row):
        return jnp.sum(jnp.where(mask, row, 0.0), axis=1, keepdims=True)

    own = lane == sub + first_row
    before = lane == sub + (first_row - 1)
    my_prob, my_deep, my_upper = pick(own, prob), pick(own, deep), pick(own, upper)
    first = lane1 == first_row
    last = lane1 == first_row + (scen_count - 1)
    first_deep, first_upper = pick(first, deep), pick(first, upper)
    last_deep, last_upper = pick(last, deep), pick(last, upper)

    def same(a, b):
        return jnp.where(a == b, 1.0, 0.0)

    section = lax.broadcasted_iota(jnp.int32, (scen_count, horizon), 1)

    def table(root, up, dp, leaf):
        return jnp.where(
            section < hours,
            root,
            jnp.where(section < 2 * hours, up, jnp.where(section < 3 * hours, dp, leaf)),
        )

    inv_root = 1.0 / jnp.sum(prob, axis=1, keepdims=True)
    inv_upper = 1.0 / pick(my_upper == upper, prob)
    inv_deep = 1.0 / pick(my_deep == deep, prob)
    inv = table(inv_root, inv_upper, inv_deep, 1.0)
    from_left = table(1.0, same(my_upper, first_upper), same(my_deep, first_deep), 0.0)
    from_right = table(1.0, same(my_upper, last_upper), same(my_deep, last_deep), 0.0)
    tab_ref[0] = table(my_prob, my_prob, my_prob, 1.0)
    tab_ref[1] = table(
        1.0, same(my_upper, pick(before, upper)), same(my_deep, pick(before, deep)), 0.0
    )
    tab_ref[2] = from_left
    tab_ref[3] = inv
    tab_ref[4] = inv * from_left
    tab_ref[5] = inv * from_right

    eye = lax.broadcasted_iota(jnp.int32, (site_count, site_count), 0) == (
        lax.broadcasted_iota(jnp.int32, (site_count, site_count), 1)
    )

    def column(ref):
        return pick(eye, ref[...].reshape(1, site_count))

    pen = column(pen_ref)
    step = 0.5 / (1.0 + pen)
    wide = (site_count, horizon)
    sites_all = site_count * n_site
    col_ref[0] = jnp.broadcast_to(pen, wide)
    col_ref[1] = jnp.broadcast_to(step, wide)
    col_ref[2] = jnp.broadcast_to(step * column(soc_ref) / (horizon * horizon), wide)
    col_out[0] = jnp.broadcast_to(step * (2.0 / sites_all), wide)
    col_out[1] = jnp.broadcast_to(column(cap_ref), wide)
    hour_a = lax.broadcasted_iota(jnp.int32, (horizon, horizon), 0)
    hour_b = lax.broadcasted_iota(jnp.int32, (horizon, horizon), 1)
    kern_ref[...] = (horizon - jnp.maximum(hour_a, hour_b)).astype(jnp.float32).astype(kern_ref.dtype)

    def ahead_of(ref, c):
        flat = ref[rows(c)].reshape(step_rows * site_count, horizon)
        if kern_ref.dtype == jnp.bfloat16:
            high = flat.astype(jnp.bfloat16)
            low = (flat - high.astype(jnp.float32)).astype(jnp.bfloat16)
            ahead = jnp.dot(high, kern_ref[...], preferred_element_type=jnp.float32) + jnp.dot(
                low, kern_ref[...], preferred_element_type=jnp.float32
            )
        else:
            ahead = jnp.dot(flat, kern_ref[...], precision=lax.Precision.HIGHEST)
        return ahead.reshape(step_rows, site_count, horizon)

    def row(ref, s):
        return ref[pl.ds(s, 1), :]

    fore = None
    first_sum = None
    for c in range(CHUNKS):
        ins[c][0].wait()
        for s in range(c * step_rows, (c + 1) * step_rows):
            x = x_ref[s]
            weighted = x * row(tab_ref.at[0], s)
            fore = weighted if fore is None else weighted + row(tab_ref.at[1], s) * fore
            floc_ref[s] = fore
            part = weighted * row(tab_ref.at[2], s)
            first_sum = part if first_sum is None else first_sum + part

    half_lane = lax.broadcasted_iota(jnp.int32, (site_count // 2, half), 1)

    def fill(slot, value):
        pay_ref[slot] = value[:, :half]
        tail = value[:, half:]
        payd_ref[slot] = jnp.where(
            half_lane < hours,
            tail[: site_count // 2],
            pltpu.roll(tail[site_count // 2 :], hours, axis=1),
        )

    fill(0, fore)
    fill(1, first_sum)

    pl.semaphore_wait(barrier, n_scen + n_site - 2)

    scen_copies = []
    for j in range(1, n_scen):
        peer = lax.rem(me + j, n_scen)
        side = jnp.where(peer > me, 0, 1)
        scen_copies.append(
            pltpu.make_async_remote_copy(
                src_ref=pay_ref.at[side],
                dst_ref=got_ref.at[j - 1],
                send_sem=scen_send.at[j - 1],
                recv_sem=scen_recv.at[j - 1],
                device_id={"scen": peer},
                device_id_type=MESH,
            )
        )
    deep_copies = []
    for side, peer in ((0, jnp.minimum(me + 1, n_scen - 1)), (1, jnp.maximum(me - 1, 0))):
        deep_copies.append(
            pltpu.make_async_remote_copy(
                src_ref=payd_ref.at[side],
                dst_ref=gotd_ref.at[side],
                send_sem=deep_send.at[side],
                recv_sem=deep_recv.at[side],
                device_id={"scen": peer},
                device_id_type=MESH,
            )
        )
    has_right = me < n_scen - 1
    has_left = me > 0

    def site_copies(turn, lanes, index):
        return [
            pltpu.make_async_remote_copy(
                src_ref=imb_ref.at[turn, :, lanes],
                dst_ref=imbr_ref.at[turn, j - 1, :, lanes],
                send_sem=site_send.at[index, j - 1],
                recv_sem=site_recv.at[index, j - 1],
                device_id={"site": lax.rem(here + j, n_site)},
                device_id_type=MESH,
            )
            for j in range(1, n_site)
        ]

    for copy in scen_copies:
        copy.start()

    @pl.when(has_right)
    def _():
        deep_copies[0].start()

    @pl.when(has_left)
    def _():
        deep_copies[1].start()


    for c in range(CHUNKS):
        ins[c][1].wait()
        for s in range(c * step_rows, (c + 1) * step_rows):
            load_total = jnp.sum(load_ref[s].astype(jnp.float32), axis=0, keepdims=True)
            loadsum_ref[pl.ds(s, 1), :] = load_total
            imb_ref[0, pl.ds(s, 1), :] = jnp.sum(x_ref[s], axis=0, keepdims=True) - load_total
    sites_first = site_copies(0, pl.ds(0, horizon), 0)
    for copy in sites_first:
        copy.start()

    energy_in.wait()
    fin_ref[0] = col_ref[1] * energy_ref[...]
    back = None
    for s in reversed(range(scen_count)):
        if back is None:
            back = floc_ref[s]
        else:
            back = jnp.where(row(tab_ref.at[1], s + 1) > 0.5, back, floc_ref[s])
        q_ref[s] = col_ref[0] * (x_ref[s] - back * row(tab_ref.at[3], s))
    for c in range(CHUNKS):
        ahead = ahead_of(x_ref, c)
        dual_in[c].wait()
        for i in range(step_rows):
            s = c * step_rows + i
            z_ref[s] = x_ref[s] - fin_ref[0] - col_ref[1] * dual_ref[s] - col_ref[2] * ahead[i]

    left = jnp.zeros((site_count, half), jnp.float32)
    right = jnp.zeros((site_count, half), jnp.float32)
    front_lane = lax.broadcasted_iota(jnp.int32, (1, half), 1)
    gates = []
    for j in range(1, n_scen):
        peer = lax.rem(me + (n_scen - j), n_scen)
        peer_last = lane1 == peer * scen_count + (scen_count - 1)
        peer_first = lane1 == peer * scen_count
        is_left = jnp.where(peer < me, 1.0, 0.0)
        gates.append(
            (
                is_left * jnp.where(front_lane < hours, 1.0, same(pick(peer_last, upper), first_upper)),
                (1.0 - is_left)
                * jnp.where(front_lane < hours, 1.0, same(pick(peer_first, upper), last_upper)),
            )
        )
    gate_left = same(pick(lane1 == first_row - 1, deep), first_deep)
    gate_right = same(pick(lane1 == first_row + scen_count, deep), last_deep)

    def unpack(value):
        return jnp.concatenate([value, pltpu.roll(value, hours, axis=1)], axis=0)

    for copy in sites_first:
        copy.wait_recv()
    imb_one = imb_ref[0]
    for j in range(n_site - 1):
        imb_one = imb_one + imbr_ref[0, j]
    tab_ref[0] = imb_one

    def update(lanes):
        for s in range(scen_count):
            spot = pl.ds(s, 1)
            q = (
                q_ref[s, :, lanes]
                - tab_ref[4, spot, lanes] * fin_ref[1, :, lanes]
                - tab_ref[5, spot, lanes] * fin_ref[2, :, lanes]
            )
            nd_ref[s, :, lanes] = dual_ref[s, :, lanes] + q
            cap = col_out[1, :, lanes]
            new = (
                z_ref[s, :, lanes]
                - 2.0 * col_ref[1, :, lanes] * q
                - col_out[0, :, lanes] * tab_ref[0, spot, lanes]
            )
            new = jnp.minimum(jnp.maximum(new, -cap), cap)
            cur_ref[s, :, lanes] = new
            imb_ref[1, spot, lanes] = (
                jnp.sum(new, axis=0, keepdims=True) - loadsum_ref[spot, lanes]
            )

    @pl.when(has_left)
    def _():
        deep_copies[0].wait_recv()

    @pl.when(has_right)
    def _():
        deep_copies[1].wait_recv()

    late, early = pl.ds(half, half), pl.ds(0, half)
    fin_ref[1, :, late] = col_ref[0, :, late] * (gate_left * unpack(gotd_ref[0]))
    fin_ref[2, :, late] = col_ref[0, :, late] * (gate_right * unpack(gotd_ref[1]))
    update(late)
    sites_late = site_copies(1, late, 1)
    for copy in sites_late:
        copy.start()

    for j in range(1, n_scen):
        scen_copies[j - 1].wait_recv()
        got = got_ref[j - 1]
        left = left + gates[j - 1][0] * got
        right = right + gates[j - 1][1] * got
    fin_ref[1, :, early] = col_ref[0, :, early] * left
    fin_ref[2, :, early] = col_ref[0, :, early] * right
    update(early)
    sites_early = site_copies(1, early, 2)
    for copy in sites_early:
        copy.start()
    sites_second = sites_late + sites_early

    for c in range(CHUNKS):
        ahead = ahead_of(cur_ref, c)
        for i in range(step_rows):
            s = c * step_rows + i
            now = cur_ref[s]
            z_ref[s] = (
                now
                - fin_ref[0]
                - col_ref[1]
                * (2.0 * nd_ref[s] - dual_ref[s] + col_ref[0] * (now - x_ref[s]))
                - col_ref[2] * ahead[i]
            )

    for copy in sites_second:
        copy.wait_recv()
    imb_two = imb_ref[1]
    for j in range(n_site - 1):
        imb_two = imb_two + imbr_ref[1, j]
    imb_out[...] = imb_two

    for copy in scen_copies + sites_first + sites_second:
        copy.wait_send()

    @pl.when(has_right)
    def _():
        deep_copies[0].wait_send()

    @pl.when(has_left)
    def _():
        deep_copies[1].wait_send()


def finish(z_ref, nd_ref, imb_ref, col_ref, out_hbm, ndual_hbm, new_ref, out_sem):
    scen_count = z_ref.shape[0]
    step_rows = scen_count // CHUNKS
    outs = [pltpu.make_async_copy(nd_ref, ndual_hbm, out_sem.at[CHUNKS])]
    outs[0].start()
    cap = col_ref[1]
    for c in range(CHUNKS):
        for s in range(c * step_rows, (c + 1) * step_rows):
            new = z_ref[s] - col_ref[0] * imb_ref[pl.ds(s, 1), :]
            new_ref[s] = jnp.minimum(jnp.maximum(new, -cap), cap)
        part = pl.ds(c * step_rows, step_rows)
        copy = pltpu.make_async_copy(new_ref.at[part], out_hbm.at[part], out_sem.at[c])
        copy.start()
        outs.append(copy)
    for copy in outs:
        copy.wait()


def body(
    n_scen,
    n_site,
    dispatch,
    dual_price,
    net_load,
    energy_price,
    penalty,
    soc_weight,
    capacity,
    probability,
    node_deep,
):
    scen_count, site_count, horizon = dispatch.shape
    f32 = jnp.float32
    full = (scen_count, site_count, horizon)
    half = horizon // 2
    vmem = pltpu.VMEM
    hbm_spec = pl.BlockSpec(memory_space=pltpu.HBM)
    vmem_spec = pl.BlockSpec(memory_space=vmem)
    kern_type = jnp.bfloat16 if horizon <= 256 else f32
    dma = pltpu.SemaphoreType.DMA
    shape = jax.ShapeDtypeStruct
    big = [
        pltpu.with_memory_space_constraint(x, pltpu.HBM)
        for x in (dispatch, dual_price, net_load, energy_price, penalty, soc_weight, capacity, probability, node_deep)
    ]
    parts = pl.pallas_call(
        functools.partial(kernel, n_scen, n_site),
        out_shape=(
            shape(full, f32),
            shape(full, f32),
            shape((scen_count, horizon), f32),
            shape((2, site_count, horizon), f32),
        ),
        in_specs=[hbm_spec] * 9,
        out_specs=(vmem_spec,) * 4,
        scratch_shapes=[
            vmem(penalty.shape, f32),
            vmem(penalty.shape, f32),
            vmem(penalty.shape, f32),
            vmem(probability.shape, f32),
            vmem(node_deep.shape, node_deep.dtype),
            vmem(full, f32),
            vmem(full, f32),
            vmem(full, net_load.dtype),
            vmem((site_count, horizon), f32),
            vmem(full, f32),
            vmem(full, f32),
            vmem(full, f32),
            vmem((3, site_count, horizon), f32),
            vmem((horizon, horizon), kern_type),
            vmem((6, scen_count, horizon), f32),
            vmem((3, site_count, horizon), f32),
            vmem((2, site_count, half), f32),
            vmem((2, site_count // 2, half), f32),
            vmem((n_scen - 1, site_count, half), f32),
            vmem((2, site_count // 2, half), f32),
            vmem((2, scen_count, horizon), f32),
            vmem((2, n_site - 1, scen_count, horizon), f32),
            vmem((scen_count, horizon), f32),
            dma((4, CHUNKS)),
            dma((5,)),
            dma((n_scen - 1,)),
            dma((n_scen - 1,)),
            dma((2,)),
            dma((2,)),
            dma((3, n_site - 1)),
            dma((3, n_site - 1)),
        ],
        compiler_params=pltpu.CompilerParams(
            collective_id=0, has_side_effects=True, vmem_limit_bytes=24 * 1024 * 1024
        ),
    )(*big)
    return pl.pallas_call(
        finish,
        out_shape=(shape(full, f32), shape(full, f32)),
        in_specs=[vmem_spec] * 4,
        out_specs=(hbm_spec, hbm_spec),
        scratch_shapes=[vmem(full, f32), dma((CHUNKS + 1,))],
        compiler_params=pltpu.CompilerParams(vmem_limit_bytes=24 * 1024 * 1024),
    )(*parts)


def solution(mesh):
    in_specs = (
        P(("group", "scen"), "site", None),
        P(("group", "scen"), "site", None),
        P(("group", "scen"), "site", None),
        P(("group", "site"), None),
        P("site"),
        P("site"),
        P("site"),
        P("group"),
        P("group"),
    )
    out_specs = (P(("group", "scen"), "site", None), P(("group", "scen"), "site", None))
    return jax.shard_map(
        functools.partial(body, mesh.shape["scen"], mesh.shape["site"]),
        mesh=mesh,
        in_specs=in_specs,
        out_specs=out_specs,
        check_vma=False,
    )
```
